32 devices in a mesh: slab: 16 (over z, x, core), strip: 2 (over y).
Axes of the slice: x: 2, y: 2, z: 4, core: 2. Of those that a mesh axis runs over, the one named last changes fastest.
Arguments:
- query_rows: bfloat16 [128, 48, 4096], P('slab', 'strip'), may hold values from -8 to 8
- key_rows: bfloat16 [128, 48, 4096], P('slab', 'strip'), may hold values from -8 to 8
- value_rows: bfloat16 [128, 48, 4096], P('slab', 'strip'), may hold values from -6 to 6
- window_offsets: int32 [8, 3], replicated, may hold values from -1 to 1, as said below
Outputs:
- attended: bfloat16 [128, 48, 4096], P('slab', 'strip')
The draws below stay inside these ranges and needn't reach their ends.
Inputs may be any that keep to these rules, and one draw needn't show every extreme that they name: `window_offsets`: each row is a tile offset (dt, dh, dw); the 8 rows are distinct, one of them is (0, 0, 0), some row has dt = -1 and some row has dt = 1.
All inputs are finite; a program needn't handle non-finite values.
Results may differ from the reference program's by a relative error of at most 0.0049.
Values may be sent and summed in bfloat16 or wider, within the bound.
A program may use at most 128 MiB of HBM per device.

```python
import jax
import jax.numpy as jnp
from jax import lax

HEADS = 32
HD = 128
TILE_T = 4
TILE_H = 8
TILE_W = 8
WIN = 8
HEIGHT = 16
WIDTH = 48
FRAMES = 8
LINES = 128


def draw_query_rows(key, part):
    line_count = FRAMES * HEIGHT
    full_shape = (line_count, WIDTH, HEADS * HD)
    return jnp.clip(jax.random.normal(jax.random.fold_in(key, 13), full_shape, jnp.float32), -8.0, 8.0).astype(jnp.bfloat16)


def draw_key_rows(key, part):
    line_count = FRAMES * HEIGHT
    full_shape = (line_count, WIDTH, HEADS * HD)
    return jnp.clip(jax.random.normal(jax.random.fold_in(key, 11), full_shape, jnp.float32), -8.0, 8.0).astype(jnp.bfloat16)


def draw_window_offsets(key, part):
    shuffled = jax.random.permutation(jax.random.fold_in(key, 21), 27)
    positions = jnp.argsort(shuffled, stable=True).astype(jnp.int32)
    code_list = jnp.arange(27, dtype=jnp.int32)
    early_minus = jnp.argmin(jnp.where(code_list < 9, positions, 99)).astype(jnp.int32)
    early_plus = jnp.argmin(jnp.where(code_list >= 18, positions, 99)).astype(jnp.int32)
    priority = positions + 100
    priority = jnp.where(code_list == 13, 0, priority)
    priority = jnp.where(code_list == early_minus, 1, priority)
    priority = jnp.where(code_list == early_plus, 2, priority)
    picked = jnp.argsort(priority, stable=True)[:WIN].astype(jnp.int32)
    picked = picked[jax.random.permutation(jax.random.fold_in(key, 23), WIN)]
    offset_rows = jnp.stack([picked // 9 - 1, picked // 3 % 3 - 1, picked % 3 - 1], axis=1)
    return offset_rows.astype(jnp.int32)


def steps_of(key, dims, split, low, high):
    loudness, own = 1.0, jax.random.fold_in(key, 6)
    for dim, shards_of in split:
        steps = jnp.exp(jax.random.uniform(jax.random.fold_in(own, dim), (shards_of,), jnp.float32, low / len(split), high / len(split)))
        loudness = loudness * jnp.repeat(steps, dims[dim] // shards_of).reshape([-1 if axis == dim else 1 for axis in range(len(dims))])
    return loudness


def scatter_about(stream_key, shape, scale, most, split=(), held_as=jnp.bfloat16):
    result = scale * jax.random.normal(stream_key, shape, jnp.float32)
    if split:
        result = result * steps_of(stream_key, shape, split, -0.22, 0.18)
    return jnp.clip(result, -most, most).astype(held_as)


def setup_inputs(seed: int = 0) -> dict:
    splits = jax.random.split(jax.random.key(seed), 5)
    query_rows = draw_query_rows(jax.random.fold_in(splits[4], 71), 0)
    key_rows = draw_key_rows(jax.random.fold_in(splits[4], 71), 0)
    value_rows = scatter_about(splits[2], (LINES, WIDTH, HEADS * HD), 1.0, 6.0, ((0, 16), (1, 2)))
    window_offsets = draw_window_offsets(jax.random.fold_in(splits[4], 71), 0)
    return dict(query_rows=query_rows, key_rows=key_rows, value_rows=value_rows, window_offsets=window_offsets)


def tile_major(field):
    shaped = field.reshape(FRAMES // TILE_T, TILE_T, HEIGHT // TILE_H, TILE_H, WIDTH // TILE_W, TILE_W, HEADS, HD)
    shaped = shaped.transpose(6, 0, 2, 4, 1, 3, 5, 7)
    return shaped.reshape(HEADS, FRAMES // TILE_T, HEIGHT // TILE_H, WIDTH // TILE_W, TILE_T * TILE_H * TILE_W, HD)


def reference(query_rows, key_rows, value_rows, window_offsets):
    frame_tiles = FRAMES // TILE_T
    row_tiles = HEIGHT // TILE_H
    col_tiles = WIDTH // TILE_W
    tokens = TILE_T * TILE_H * TILE_W
    padding = ((0, 0), (1, 1), (1, 1), (1, 1), (0, 0), (0, 0))
    query_tiles = tile_major(query_rows)
    key_tiles = jnp.pad(tile_major(key_rows), padding)
    value_tiles = jnp.pad(tile_major(value_rows), padding)
    grid_shape = (frame_tiles, row_tiles, col_tiles, WIN)
    key_frame = jnp.broadcast_to(jnp.arange(frame_tiles, dtype=jnp.int32)[:, None, None, None] + window_offsets[:, 0], grid_shape)
    key_row = jnp.broadcast_to(jnp.arange(row_tiles, dtype=jnp.int32)[None, :, None, None] + window_offsets[:, 1], grid_shape)
    key_col = jnp.broadcast_to(jnp.arange(col_tiles, dtype=jnp.int32)[None, None, :, None] + window_offsets[:, 2], grid_shape)
    inside = (key_frame >= 0) & (key_frame < frame_tiles) & (key_row >= 0) & (key_row < row_tiles)
    inside = inside & (key_col >= 0) & (key_col < col_tiles)
    score_scale = HD ** -0.5

    def one_head(tensors):
        query_head, key_head, value_head = tensors

        def one_layer(layer_index):
            query_layer = lax.dynamic_index_in_dim(query_head, layer_index, 0, keepdims=False).astype(jnp.float32)
            frame_pick = lax.dynamic_index_in_dim(key_frame, layer_index, 0, keepdims=False) + 1
            row_pick = lax.dynamic_index_in_dim(key_row, layer_index, 0, keepdims=False) + 1
            col_pick = lax.dynamic_index_in_dim(key_col, layer_index, 0, keepdims=False) + 1
            live_tiles = lax.dynamic_index_in_dim(inside, layer_index, 0, keepdims=False)
            window_keys = key_head[frame_pick, row_pick, col_pick].reshape(row_tiles, col_tiles, WIN * tokens, HD).astype(jnp.float32)
            window_values = value_head[frame_pick, row_pick, col_pick].reshape(row_tiles, col_tiles, WIN * tokens, HD).astype(jnp.float32)
            scores = jnp.einsum("hwqd,hwkd->hwqk", query_layer, window_keys) * score_scale
            key_live = jnp.repeat(live_tiles, tokens, axis=2)
            scores = jnp.where(key_live[:, :, None, :], scores, -1e30)
            row_max = jnp.max(scores, axis=-1, keepdims=True)
            raised = jnp.exp(scores - row_max)
            weights = (raised / jnp.sum(raised, axis=-1, keepdims=True)).astype(jnp.bfloat16)
            weights = lax.optimization_barrier(weights)
            mixed_out = jnp.einsum("hwqk,hwkd->hwqd", weights.astype(jnp.float32), window_values)
            return mixed_out.astype(jnp.bfloat16)

        return lax.map(one_layer, jnp.arange(frame_tiles, dtype=jnp.int32))

    attended = lax.map(one_head, (query_tiles, key_tiles, value_tiles))
    attended = attended.reshape(HEADS, frame_tiles, row_tiles, col_tiles, TILE_T, TILE_H, TILE_W, HD)
    attended = attended.transpose(1, 4, 2, 5, 3, 6, 0, 7)
    return attended.reshape(FRAMES * HEIGHT, WIDTH, HEADS * HD)
```

```python
import functools
import math

import jax
import jax.numpy as jnp
from jax import lax
from jax.experimental import pallas as pl
from jax.experimental.pallas import tpu as pltpu
from jax.sharding import PartitionSpec as P

HD = 128
TILE_T = 4
TILE_H = 8
TILE_W = 8


def swapped(value, axis, apart):
    mask = 2**apart
    pairs = [(source, source ^ mask) for source in range(lax.axis_size(axis))]
    return lax.ppermute(value, axis, pairs)


def from_behind(block, axis, distance):
    devices = range(lax.axis_size(axis))
    route = [(i - distance, i) for i in devices if i - distance in devices]
    return lax.ppermute(block, axis, route)


def pair_transpose(pieces, move_piece, bit_order):
    slab_pos = lax.axis_index("slab")
    shaped = pieces.reshape((2, 2, 2) + pieces.shape[1:])
    for bit_num in bit_order:
        axis_num = 2 - bit_num
        is_upper = slab_pos >> bit_num & 1 == 1
        lower_half = jnp.take(shaped, 0, axis=axis_num)
        upper_half = jnp.take(shaped, 1, axis=axis_num)
        kept_part = jnp.where(is_upper, upper_half, lower_half)
        sent_part = jnp.where(is_upper, lower_half, upper_half)
        got_part = move_piece(sent_part, bit_num)
        shaped = jnp.stack(
            [jnp.where(is_upper, got_part, kept_part), jnp.where(is_upper, kept_part, got_part)],
            axis=axis_num,
        )
    return shaped.reshape((8,) + shaped.shape[3:])


def widen_rims(own_cols, rim_cols, right_side):
    blank = jnp.zeros_like(rim_cols)
    return jnp.concatenate(
        [jnp.where(right_side, blank, rim_cols), own_cols, jnp.where(right_side, rim_cols, blank)],
        axis=-2,
    )


def send_tiles(segment, bit_num):
    return swapped(segment, "slab", bit_num)


def send_rows(segment, bit_num):
    return swapped(segment, "slab", bit_num)


def per_device(query_rows, key_rows, value_rows, window_offsets):
    bit_order = (0, 1, 2)
    line_count = query_rows.shape[0]
    stacked = jnp.stack([query_rows, key_rows, value_rows])
    by_head = lax.all_to_all(stacked, "strip", split_axis=3, concat_axis=2, tiled=True)
    full_width = by_head.shape[2]
    half_width = full_width // 2
    piece_width = by_head.shape[3] // 4
    device_heads = piece_width // HD
    pieces = by_head.reshape(3, line_count, 2, half_width, 4, piece_width).transpose(
        2, 4, 0, 1, 3, 5
    )
    pieces = pieces.reshape(8, 3, line_count, half_width, piece_width)
    arrived = pair_transpose(pieces, send_tiles, bit_order)
    tile_block = arrived.reshape(TILE_T, 2, 3, line_count, half_width, piece_width).transpose(
        2, 0, 1, 3, 4, 5
    )
    tile_block = tile_block.reshape(3, TILE_T, 2 * line_count, half_width, piece_width)
    query_block = tile_block[0]
    key_value = tile_block[1:]
    slab_pos = lax.axis_index("slab")
    frame_tile = slab_pos // 8
    side_half = slab_pos // 4 % 2
    right_side = side_half == 0
    edge_cols = jnp.where(
        right_side, key_value[..., half_width - TILE_W :, :], key_value[..., :TILE_W, :]
    )
    rim_cols = swapped(edge_cols, "slab", 2)
    carried = jnp.concatenate([key_value, rim_cols], axis=-2)
    earlier_layer = from_behind(carried, "slab", 8)
    later_layer = from_behind(carried, "slab", -8)
    extended = jnp.stack(
        [
            widen_rims(layer_data[..., :half_width, :], layer_data[..., half_width:, :], right_side)
            for layer_data in (earlier_layer, carried, later_layer)
        ]
    )
    tile_rows = 2 * line_count // TILE_H
    tile_cols = half_width // TILE_W
    wide_cols = tile_cols + 2
    tokens = TILE_T * TILE_H * TILE_W
    key_tiles = extended.reshape(
        3, 2, TILE_T, tile_rows, TILE_H, wide_cols, TILE_W, device_heads, HD
    )
    key_tiles = key_tiles.transpose(0, 3, 5, 1, 2, 4, 6, 7, 8).reshape(
        3 * tile_rows * wide_cols, 2, tokens, device_heads, HD
    )
    query_tiles = query_block.reshape(
        TILE_T, tile_rows, TILE_H, tile_cols, TILE_W, device_heads, HD
    )
    query_tiles = query_tiles.transpose(1, 3, 0, 2, 4, 5, 6).reshape(
        tile_rows * tile_cols, tokens, device_heads, HD
    )
    query_count = tile_rows * tile_cols
    window_count = window_offsets.shape[0]
    tile_ids = jnp.arange(query_count, dtype=jnp.int32)
    row_tile = (tile_ids // tile_cols)[:, None]
    col_local = (tile_ids % tile_cols)[:, None]
    shift_frame = window_offsets[:, 0][None, :]
    shift_row = window_offsets[:, 1][None, :]
    shift_col = window_offsets[:, 2][None, :]
    key_frame = frame_tile + shift_frame
    key_row = row_tile + shift_row
    key_col = side_half * tile_cols + col_local + shift_col
    frame_total = lax.axis_size("slab") // 8
    inside = (key_frame >= 0) & (key_frame < frame_total) & (key_row >= 0) & (key_row < tile_rows)
    inside = inside & (key_col >= 0) & (key_col < 2 * tile_cols)
    flat_index = (
        (1 + shift_frame) * (tile_rows * wide_cols)
        + jnp.clip(key_row, 0, tile_rows - 1) * wide_cols
        + 1
        + col_local
        + shift_col
    )
    tiles_step = min(query_count, max(1, 512 // tokens))
    step_count = query_count // tiles_step
    score_scale = HD ** (-0.5)

    def attend(inputs):
        query_tile, tile_index, tile_live = inputs
        window_tiles = jnp.take(key_tiles, tile_index.reshape(-1), axis=0)
        window_tiles = window_tiles.reshape(tiles_step, window_count, 2, tokens, device_heads, HD)
        window_keys = window_tiles[:, :, 0].reshape(
            tiles_step, window_count * tokens, device_heads, HD
        )
        window_values = window_tiles[:, :, 1].reshape(
            tiles_step, window_count * tokens, device_heads, HD
        )
        scores = jnp.einsum(
            "pqhd,pkhd->phqk", query_tile, window_keys, preferred_element_type=jnp.float32
        )
        key_live = jnp.repeat(tile_live, tokens, axis=1)
        scores = jnp.where(key_live[:, None, None, :], scores, -1e30)
        row_max = jnp.max(scores, axis=-1, keepdims=True)
        raised = jnp.exp((scores - row_max) * score_scale)
        weights = (raised / jnp.sum(raised, axis=-1, keepdims=True)).astype(jnp.bfloat16)
        mixed_out = jnp.einsum(
            "phqk,pkhd->pqhd", weights, window_values, preferred_element_type=jnp.float32
        )
        return mixed_out.astype(jnp.bfloat16)

    attended = lax.map(
        attend,
        (
            query_tiles.reshape(step_count, tiles_step, tokens, device_heads, HD),
            flat_index.reshape(step_count, tiles_step, window_count),
            inside.reshape(step_count, tiles_step, window_count),
        ),
    )
    attended = attended.reshape(tile_rows, tile_cols, TILE_T, TILE_H, TILE_W, device_heads, HD)
    attended = attended.transpose(2, 0, 3, 1, 4, 5, 6).reshape(
        8, line_count, half_width, piece_width
    )
    returned = pair_transpose(attended, send_rows, bit_order)
    merged = returned.reshape(2, 4, line_count, half_width, piece_width).transpose(2, 0, 3, 1, 4)
    merged = merged.reshape(line_count, full_width, 4 * piece_width)
    return lax.all_to_all(merged, "strip", split_axis=1, concat_axis=2, tiled=True)


BY = 4
FT = TILE_T
COLS = 3
ROW_TILES = 2
COL_TILES = 6
TOKENS = TILE_T * TILE_H * TILE_W


def head_kernel(layers, windows, off_ref, q_ref, k_ref, v_ref, out_ref, kv_in, q_in, o_buf,
                k_tiles, v_tiles, q_wide, o_wide, kv_sems, q_sems, out_sem, kv_sent, q_sent,
                o_sent):
    devices = layers * FT * BY
    tiles = layers * ROW_TILES * COL_TILES
    me = lax.axis_index("slab") * 2 + lax.axis_index("strip")
    layer, frame, lane = me // (FT * BY), me // BY % FT, me % BY

    def mesh_id(device):
        return (device // 2, device % 2)

    def device_of(a, f, b):
        return (a * FT + f) * BY + b

    def columns(device):
        return pl.ds(pl.multiple_of(device * HD, HD), HD)

    barrier = pltpu.get_barrier_semaphore()

    @pl.loop(1, devices)
    def _(i):
        pl.semaphore_signal(
            barrier, inc=1, device_id=mesh_id((me + i) % devices),
            device_id_type=pl.DeviceIdType.MESH,
        )

    pl.semaphore_wait(barrier, devices - 1)

    def kv_step(i):
        return (layers - 1) - i % layers, i // layers % FT, i // (layers * FT)

    def q_step(i):
        return (layers - 1) - i // FT % layers, i % FT, i // (layers * FT)

    def ahead(step):
        a, f, b = step
        return device_of((layer + a) % layers, (frame + f) % FT, (lane + b) % BY)

    kv_self = layers - 1
    q_self = (layers - 1) * FT
    my_group = layer * BY + lane

    pltpu.make_async_copy(k_ref.at[:, columns(me)], kv_in.at[me, 0], kv_sems.at[me]).start()
    pltpu.make_async_copy(v_ref.at[:, columns(me)], kv_in.at[me, 1], kv_sems.at[me]).start()
    pltpu.make_async_copy(
        q_ref.at[:, columns(me)], q_in.at[my_group, frame], q_sems.at[my_group]
    ).start()

    def send_kv(i):
        to = ahead(kv_step(i))
        for part, ref in enumerate((k_ref, v_ref)):
            pltpu.make_async_remote_copy(
                src_ref=ref.at[:, columns(to)],
                dst_ref=kv_in.at[me, part],
                send_sem=kv_sent,
                recv_sem=kv_sems.at[me],
                device_id=mesh_id(to),
                device_id_type=pl.DeviceIdType.MESH,
            ).start()

    def send_q(i):
        to = ahead(q_step(i))
        pltpu.make_async_remote_copy(
            src_ref=q_ref.at[:, columns(to)],
            dst_ref=q_in.at[my_group, frame],
            send_sem=q_sent,
            recv_sem=q_sems.at[my_group],
            device_id=mesh_id(to),
            device_id_type=pl.DeviceIdType.MESH,
        ).start()

    for send, own in ((send_kv, kv_self), (send_q, q_self)):
        pl.loop(0, own)(send)
        pl.loop(own + 1, devices)(send)

    @pl.loop(0, tiles)
    def _(t):
        v_tiles[t, :, :, HD:] = jnp.ones((FT, 64, HD), jnp.bfloat16)

    v_tiles[tiles] = jnp.zeros((FT, 64, 2 * HD), jnp.bfloat16)

    @pl.loop(0, devices)
    def _(i):
        a, f, b = kv_step(i)
        a, f, b = (layer + layers - a) % layers, (frame + FT - f) % FT, (lane + BY - b) % BY
        source = device_of(a, f, b)
        pltpu.make_async_copy(kv_in.at[source], kv_in.at[source], kv_sems.at[source]).wait()
        first = (a * ROW_TILES + b // 2) * COL_TILES + b % 2 * COLS
        key_block = kv_in[source, 0].astype(jnp.float32).reshape(TILE_H, COLS, TILE_W, HD)
        value_block = kv_in[source, 1].astype(jnp.float32).reshape(TILE_H, COLS, TILE_W, HD)
        for c in range(COLS):
            k_tiles[first + c, f] = key_block[:, c].reshape(64, HD).astype(jnp.bfloat16)
            v_tiles[first + c, f, :, :HD] = (
                value_block[:, c].reshape(64, HD).astype(jnp.bfloat16)
            )

    factor = HD ** (-0.5) * math.log2(math.e)

    @pl.loop(0, layers * BY)
    def _(n):
        a = (layer + layers - ((layers - 1) - n % layers)) % layers
        b = (lane + BY - n // layers) % BY
        group = a * BY + b
        pltpu.make_async_copy(q_in.at[group], q_in.at[group], q_sems.at[group]).wait()
        q_wide[...] = q_in[group].astype(jnp.float32).reshape(FT, TILE_H, COLS, TILE_W, HD)

        @pl.loop(0, COLS)
        def _(c):
            row, col = b // 2, b % 2 * COLS + c
            own = (a * ROW_TILES + row) * COL_TILES + col
            query = q_wide[:, :, c].reshape(TOKENS, HD).astype(jnp.bfloat16)
            scores, picks = [], []
            for w in range(windows):
                ka, kr, kc = a + off_ref[w, 0], row + off_ref[w, 1], col + off_ref[w, 2]
                live = (ka >= 0) & (ka < layers) & (kr >= 0) & (kr < ROW_TILES)
                live = live & (kc >= 0) & (kc < COL_TILES)
                tile = (ka * ROW_TILES + kr) * COL_TILES + kc
                picks.append(jnp.where(live, tile, tiles))
                keys = k_tiles[jnp.where(live, tile, own)].reshape(TOKENS, HD)
                scores.append(
                    lax.dot_general(
                        query, keys, (((1,), (1,)), ((), ())),
                        preferred_element_type=jnp.float32,
                    )
                )
            top = functools.reduce(jnp.maximum, scores)
            top = jnp.max(top, axis=-1, keepdims=True)
            total = jnp.zeros((TOKENS, 2 * HD), jnp.float32)
            for score, pick in zip(scores, picks):
                raised = jnp.exp2((score - top) * factor).astype(jnp.bfloat16)
                values = v_tiles[pick].reshape(TOKENS, 2 * HD)
                total += jnp.dot(raised, values, preferred_element_type=jnp.float32)
            mixed = total[:, :HD] / total[:, HD:]
            o_wide[:, :, c] = mixed.reshape(FT, TILE_H, TILE_W, HD)

        o_buf[group] = o_wide[...].reshape(FT, 192, HD).astype(jnp.bfloat16)

        @pl.loop(0, FT)
        def _(f):
            to = device_of(a, f, b)

            @pl.when(to == me)
            def _():
                pltpu.make_async_copy(
                    o_buf.at[group, f], out_ref.at[:, columns(me)], out_sem
                ).start()

            @pl.when(to != me)
            def _():
                pltpu.make_async_remote_copy(
                    src_ref=o_buf.at[group, f],
                    dst_ref=out_ref.at[:, columns(me)],
                    send_sem=o_sent,
                    recv_sem=out_sem,
                    device_id=mesh_id(to),
                    device_id_type=pl.DeviceIdType.MESH,
                ).start()

    others = pl.ds(0, devices - 1)
    pltpu.make_async_copy(kv_in.at[others], kv_in.at[others], kv_sent).wait()
    sent = kv_in.at[others, 0]
    pltpu.make_async_copy(sent, sent, q_sent).wait()
    pltpu.make_async_copy(sent, sent, o_sent).wait()
    pltpu.make_async_copy(out_ref, out_ref, out_sem).wait()


def by_head(query_rows, key_rows, value_rows, window_offsets):
    shape = query_rows.shape
    devices = lax.axis_size("slab") * lax.axis_size("strip")
    layers = devices // (FT * BY)
    tiles = layers * ROW_TILES * COL_TILES
    windows = window_offsets.shape[0]
    tokens, width = shape[0] * shape[1], shape[2]
    flat = [x.reshape(tokens, width) for x in (query_rows, key_rows, value_rows)]
    pairs = tiles * windows * TOKENS * TOKENS
    out = pl.pallas_call(
        functools.partial(head_kernel, layers, windows),
        out_shape=jax.ShapeDtypeStruct((tokens, width), jnp.bfloat16),
        in_specs=[pl.BlockSpec(memory_space=pltpu.SMEM)]
        + [pl.BlockSpec(memory_space=pl.ANY)] * 3,
        out_specs=pl.BlockSpec(memory_space=pl.ANY),
        scratch_shapes=[
            pltpu.VMEM((devices, 2, tokens, HD), jnp.bfloat16),
            pltpu.VMEM((layers * BY, FT, tokens, HD), jnp.bfloat16),
            pltpu.VMEM((layers * BY, FT, tokens, HD), jnp.bfloat16),
            pltpu.VMEM((tiles, FT, 64, HD), jnp.bfloat16),
            pltpu.VMEM((tiles + 1, FT, 64, 2 * HD), jnp.bfloat16),
            pltpu.VMEM((FT, TILE_H, COLS, TILE_W, HD), jnp.float32),
            pltpu.VMEM((FT, TILE_H, COLS, TILE_W, HD), jnp.float32),
            pltpu.SemaphoreType.DMA((devices,)),
            pltpu.SemaphoreType.DMA((layers * BY,)),
            pltpu.SemaphoreType.DMA,
            pltpu.SemaphoreType.DMA,
            pltpu.SemaphoreType.DMA,
            pltpu.SemaphoreType.DMA,
        ],
        compiler_params=pltpu.CompilerParams(
            collective_id=0, has_side_effects=True, vmem_limit_bytes=40 * 2**20
        ),
        cost_estimate=pl.CostEstimate(
            flops=6 * pairs * HD, bytes_accessed=8 * tokens * width, transcendentals=pairs
        ),
    )(window_offsets, *flat)
    return out.reshape(shape)


def solution(mesh):
    specs = P("slab", "strip", None)

    def attention(query_rows, key_rows, value_rows, window_offsets):
        slabs, strips = mesh.shape["slab"], mesh.shape["strip"]
        lines, width, features = query_rows.shape
        fits = slabs * strips * HD == features and lines == slabs * TILE_H
        fits = fits and strips == 2 and width == strips * COLS * TILE_W and slabs % 8 == 0
        return jax.shard_map(
            by_head if fits else per_device,
            mesh=mesh,
            in_specs=(specs, specs, specs, P()),
            out_specs=specs,
            check_vma=False,
        )(query_rows, key_rows, value_rows, window_offsets)

    return attention
```

```python
import functools
import math

import jax
import jax.numpy as jnp
from jax import lax
from jax.experimental import pallas as pl
from jax.experimental.pallas import tpu as pltpu
from jax.sharding import PartitionSpec as P

HD = 128
TILE_T = 4
TILE_H = 8
TILE_W = 8


def swapped(value, axis, apart):
    mask = 2**apart
    pairs = [(source, source ^ mask) for source in range(lax.axis_size(axis))]
    return lax.ppermute(value, axis, pairs)


def from_behind(block, axis, distance):
    devices = range(lax.axis_size(axis))
    route = [(i - distance, i) for i in devices if i - distance in devices]
    return lax.ppermute(block, axis, route)


def pair_transpose(pieces, move_piece, bit_order):
    slab_pos = lax.axis_index("slab")
    shaped = pieces.reshape((2, 2, 2) + pieces.shape[1:])
    for bit_num in bit_order:
        axis_num = 2 - bit_num
        is_upper = slab_pos >> bit_num & 1 == 1
        lower_half = jnp.take(shaped, 0, axis=axis_num)
        upper_half = jnp.take(shaped, 1, axis=axis_num)
        kept_part = jnp.where(is_upper, upper_half, lower_half)
        sent_part = jnp.where(is_upper, lower_half, upper_half)
        got_part = move_piece(sent_part, bit_num)
        shaped = jnp.stack(
            [jnp.where(is_upper, got_part, kept_part), jnp.where(is_upper, kept_part, got_part)],
            axis=axis_num,
        )
    return shaped.reshape((8,) + shaped.shape[3:])


def widen_rims(own_cols, rim_cols, right_side):
    blank = jnp.zeros_like(rim_cols)
    return jnp.concatenate(
        [jnp.where(right_side, blank, rim_cols), own_cols, jnp.where(right_side, rim_cols, blank)],
        axis=-2,
    )


def send_tiles(segment, bit_num):
    return swapped(segment, "slab", bit_num)


def send_rows(segment, bit_num):
    return swapped(segment, "slab", bit_num)


def per_device(query_rows, key_rows, value_rows, window_offsets):
    bit_order = (0, 1, 2)
    line_count = query_rows.shape[0]
    stacked = jnp.stack([query_rows, key_rows, value_rows])
    by_head = lax.all_to_all(stacked, "strip", split_axis=3, concat_axis=2, tiled=True)
    full_width = by_head.shape[2]
    half_width = full_width // 2
    piece_width = by_head.shape[3] // 4
    device_heads = piece_width // HD
    pieces = by_head.reshape(3, line_count, 2, half_width, 4, piece_width).transpose(
        2, 4, 0, 1, 3, 5
    )
    pieces = pieces.reshape(8, 3, line_count, half_width, piece_width)
    arrived = pair_transpose(pieces, send_tiles, bit_order)
    tile_block = arrived.reshape(TILE_T, 2, 3, line_count, half_width, piece_width).transpose(
        2, 0, 1, 3, 4, 5
    )
    tile_block = tile_block.reshape(3, TILE_T, 2 * line_count, half_width, piece_width)
    query_block = tile_block[0]
    key_value = tile_block[1:]
    slab_pos = lax.axis_index("slab")
    frame_tile = slab_pos // 8
    side_half = slab_pos // 4 % 2
    right_side = side_half == 0
    edge_cols = jnp.where(
        right_side, key_value[..., half_width - TILE_W :, :], key_value[..., :TILE_W, :]
    )
    rim_cols = swapped(edge_cols, "slab", 2)
    carried = jnp.concatenate([key_value, rim_cols], axis=-2)
    earlier_layer = from_behind(carried, "slab", 8)
    later_layer = from_behind(carried, "slab", -8)
    extended = jnp.stack(
        [
            widen_rims(layer_data[..., :half_width, :], layer_data[..., half_width:, :], right_side)
            for layer_data in (earlier_layer, carried, later_layer)
        ]
    )
    tile_rows = 2 * line_count // TILE_H
    tile_cols = half_width // TILE_W
    wide_cols = tile_cols + 2
    tokens = TILE_T * TILE_H * TILE_W
    key_tiles = extended.reshape(
        3, 2, TILE_T, tile_rows, TILE_H, wide_cols, TILE_W, device_heads, HD
    )
    key_tiles = key_tiles.transpose(0, 3, 5, 1, 2, 4, 6, 7, 8).reshape(
        3 * tile_rows * wide_cols, 2, tokens, device_heads, HD
    )
    query_tiles = query_block.reshape(
        TILE_T, tile_rows, TILE_H, tile_cols, TILE_W, device_heads, HD
    )
    query_tiles = query_tiles.transpose(1, 3, 0, 2, 4, 5, 6).reshape(
        tile_rows * tile_cols, tokens, device_heads, HD
    )
    query_count = tile_rows * tile_cols
    window_count = window_offsets.shape[0]
    tile_ids = jnp.arange(query_count, dtype=jnp.int32)
    row_tile = (tile_ids // tile_cols)[:, None]
    col_local = (tile_ids % tile_cols)[:, None]
    shift_frame = window_offsets[:, 0][None, :]
    shift_row = window_offsets[:, 1][None, :]
    shift_col = window_offsets[:, 2][None, :]
    key_frame = frame_tile + shift_frame
    key_row = row_tile + shift_row
    key_col = side_half * tile_cols + col_local + shift_col
    frame_total = lax.axis_size("slab") // 8
    inside = (key_frame >= 0) & (key_frame < frame_total) & (key_row >= 0) & (key_row < tile_rows)
    inside = inside & (key_col >= 0) & (key_col < 2 * tile_cols)
    flat_index = (
        (1 + shift_frame) * (tile_rows * wide_cols)
        + jnp.clip(key_row, 0, tile_rows - 1) * wide_cols
        + 1
        + col_local
        + shift_col
    )
    tiles_step = min(query_count, max(1, 512 // tokens))
    step_count = query_count // tiles_step
    score_scale = HD ** (-0.5)

    def attend(inputs):
        query_tile, tile_index, tile_live = inputs
        window_tiles = jnp.take(key_tiles, tile_index.reshape(-1), axis=0)
        window_tiles = window_tiles.reshape(tiles_step, window_count, 2, tokens, device_heads, HD)
        window_keys = window_tiles[:, :, 0].reshape(
            tiles_step, window_count * tokens, device_heads, HD
        )
        window_values = window_tiles[:, :, 1].reshape(
            tiles_step, window_count * tokens, device_heads, HD
        )
        scores = jnp.einsum(
            "pqhd,pkhd->phqk", query_tile, window_keys, preferred_element_type=jnp.float32
        )
        key_live = jnp.repeat(tile_live, tokens, axis=1)
        scores = jnp.where(key_live[:, None, None, :], scores, -1e30)
        row_max = jnp.max(scores, axis=-1, keepdims=True)
        raised = jnp.exp((scores - row_max) * score_scale)
        weights = (raised / jnp.sum(raised, axis=-1, keepdims=True)).astype(jnp.bfloat16)
        mixed_out = jnp.einsum(
            "phqk,pkhd->pqhd", weights, window_values, preferred_element_type=jnp.float32
        )
        return mixed_out.astype(jnp.bfloat16)

    attended = lax.map(
        attend,
        (
            query_tiles.reshape(step_count, tiles_step, tokens, device_heads, HD),
            flat_index.reshape(step_count, tiles_step, window_count),
            inside.reshape(step_count, tiles_step, window_count),
        ),
    )
    attended = attended.reshape(tile_rows, tile_cols, TILE_T, TILE_H, TILE_W, device_heads, HD)
    attended = attended.transpose(2, 0, 3, 1, 4, 5, 6).reshape(
        8, line_count, half_width, piece_width
    )
    returned = pair_transpose(attended, send_rows, bit_order)
    merged = returned.reshape(2, 4, line_count, half_width, piece_width).transpose(2, 0, 3, 1, 4)
    merged = merged.reshape(line_count, full_width, 4 * piece_width)
    return lax.all_to_all(merged, "strip", split_axis=1, concat_axis=2, tiled=True)


BY = 4
FT = TILE_T
COLS = 3
ROW_TILES = 2
COL_TILES = 6
TOKENS = TILE_T * TILE_H * TILE_W


def head_kernel(layers, windows, off_ref, q_ref, k_ref, v_ref, out_ref, kv_in, q_in, o_buf,
                k_tiles, v_tiles, q_wide, o_wide, kv_sems, q_sems, out_sem, kv_sent, q_sent,
                o_sent):
    devices = layers * FT * BY
    tiles = layers * ROW_TILES * COL_TILES
    me = lax.axis_index("slab") * 2 + lax.axis_index("strip")
    layer, frame, lane = me // (FT * BY), me // BY % FT, me % BY

    def mesh_id(device):
        return (device // 2, device % 2)

    def device_of(a, f, b):
        return (a * FT + f) * BY + b

    def columns(device):
        return pl.ds(pl.multiple_of(device * HD, HD), HD)

    barrier = pltpu.get_barrier_semaphore()

    @pl.loop(1, devices)
    def _(i):
        pl.semaphore_signal(
            barrier, inc=1, device_id=mesh_id((me + i) % devices),
            device_id_type=pl.DeviceIdType.MESH,
        )

    pl.semaphore_wait(barrier, devices - 1)

    def kv_step(i):
        return (layers - 1) - i % layers, i // layers % FT, i // (layers * FT)

    def group_step(n):
        return (layers - 1) - n // 2 % layers, n // (2 * layers) * 2 + n % 2

    def q_step(i):
        a, b = group_step(i // FT)
        return a, i % FT, b

    def ahead(step):
        a, f, b = step
        return device_of((layer + a) % layers, (frame + f) % FT, (lane + b) % BY)

    kv_self = layers - 1
    q_self = (layers - 1) * 2 * FT
    q_early = devices // 2
    my_group = layer * BY + lane

    pltpu.make_async_copy(k_ref.at[:, columns(me)], kv_in.at[me, 0], kv_sems.at[me]).start()
    pltpu.make_async_copy(v_ref.at[:, columns(me)], kv_in.at[me, 1], kv_sems.at[me]).start()
    pltpu.make_async_copy(
        q_ref.at[:, columns(me)], q_in.at[my_group, frame], q_sems.at[my_group]
    ).start()

    def send_kv(i):
        to = ahead(kv_step(i))
        for part, ref in enumerate((k_ref, v_ref)):
            pltpu.make_async_remote_copy(
                src_ref=ref.at[:, columns(to)],
                dst_ref=kv_in.at[me, part],
                send_sem=kv_sent,
                recv_sem=kv_sems.at[me],
                device_id=mesh_id(to),
                device_id_type=pl.DeviceIdType.MESH,
            ).start()

    def send_q(i):
        to = ahead(q_step(i))
        pltpu.make_async_remote_copy(
            src_ref=q_ref.at[:, columns(to)],
            dst_ref=q_in.at[my_group, frame],
            send_sem=q_sent,
            recv_sem=q_sems.at[my_group],
            device_id=mesh_id(to),
            device_id_type=pl.DeviceIdType.MESH,
        ).start()

    pl.loop(0, kv_self)(send_kv)
    pl.loop(kv_self + 1, devices)(send_kv)
    pl.loop(0, q_self)(send_q)
    pl.loop(q_self + 1, q_early)(send_q)

    @pl.loop(0, tiles)
    def _(t):
        v_tiles[t, :, :, HD:] = jnp.ones((FT, 64, HD), jnp.bfloat16)

    v_tiles[tiles] = jnp.zeros((FT, 64, 2 * HD), jnp.bfloat16)

    @pl.loop(0, devices)
    def _(i):
        @pl.when(i >= q_early)
        def _():
            send_q(i)

        a, f, b = kv_step(i)
        a, f, b = (layer + layers - a) % layers, (frame + FT - f) % FT, (lane + BY - b) % BY
        source = device_of(a, f, b)
        pltpu.make_async_copy(kv_in.at[source], kv_in.at[source], kv_sems.at[source]).wait()
        first = (a * ROW_TILES + b // 2) * COL_TILES + b % 2 * COLS
        key_block = kv_in[source, 0].astype(jnp.float32).reshape(TILE_H, COLS, TILE_W, HD)
        value_block = kv_in[source, 1].astype(jnp.float32).reshape(TILE_H, COLS, TILE_W, HD)
        for c in range(COLS):
            k_tiles[first + c, f] = key_block[:, c].reshape(64, HD).astype(jnp.bfloat16)
            v_tiles[first + c, f, :, :HD] = (
                value_block[:, c].reshape(64, HD).astype(jnp.bfloat16)
            )

    factor = HD ** (-0.5) * math.log2(math.e)

    @pl.loop(0, layers * BY)
    def _(n):
        a, b = group_step(n)
        a, b = (layer + layers - a) % layers, (lane + BY - b) % BY
        group = a * BY + b
        pltpu.make_async_copy(q_in.at[group], q_in.at[group], q_sems.at[group]).wait()
        q_wide[...] = q_in[group].astype(jnp.float32).reshape(FT, TILE_H, COLS, TILE_W, HD)

        @pl.loop(0, COLS)
        def _(c):
            row, col = b // 2, b % 2 * COLS + c
            own = (a * ROW_TILES + row) * COL_TILES + col
            query = q_wide[:, :, c].reshape(TOKENS, HD).astype(jnp.bfloat16)
            scores, picks = [], []
            for w in range(windows):
                ka, kr, kc = a + off_ref[0, w], row + off_ref[1, w], col + off_ref[2, w]
                live = (ka >= 0) & (ka < layers) & (kr >= 0) & (kr < ROW_TILES)
                live = live & (kc >= 0) & (kc < COL_TILES)
                tile = (ka * ROW_TILES + kr) * COL_TILES + kc
                picks.append(jnp.where(live, tile, tiles))
                keys = k_tiles[jnp.where(live, tile, own)].reshape(TOKENS, HD)
                scores.append(
                    lax.dot_general(
                        query, keys, (((1,), (1,)), ((), ())),
                        preferred_element_type=jnp.float32,
                    )
                )
            top = functools.reduce(jnp.maximum, scores)
            top = jnp.max(top, axis=-1, keepdims=True)
            total = jnp.zeros((TOKENS, 2 * HD), jnp.float32)
            for score, pick in zip(scores, picks):
                raised = jnp.exp2((score - top) * factor).astype(jnp.bfloat16)
                values = v_tiles[pick].reshape(TOKENS, 2 * HD)
                total += jnp.dot(raised, values, preferred_element_type=jnp.float32)
            mixed = total[:, :HD] / total[:, HD:]
            o_wide[:, :, c] = mixed.reshape(FT, TILE_H, TILE_W, HD)

        o_buf[group] = o_wide[...].reshape(FT, 192, HD).astype(jnp.bfloat16)

        @pl.loop(0, FT)
        def _(f):
            to = device_of(a, f, b)

            @pl.when(to == me)
            def _():
                pltpu.make_async_copy(
                    o_buf.at[group, f], out_ref.at[:, columns(me)], out_sem
                ).start()

            @pl.when(to != me)
            def _():
                pltpu.make_async_remote_copy(
                    src_ref=o_buf.at[group, f],
                    dst_ref=out_ref.at[:, columns(me)],
                    send_sem=o_sent,
                    recv_sem=out_sem,
                    device_id=mesh_id(to),
                    device_id_type=pl.DeviceIdType.MESH,
                ).start()

    others = pl.ds(0, devices - 1)
    pltpu.make_async_copy(kv_in.at[others], kv_in.at[others], kv_sent).wait()
    sent = kv_in.at[others, 0]
    pltpu.make_async_copy(sent, sent, q_sent).wait()
    pltpu.make_async_copy(sent, sent, o_sent).wait()
    pltpu.make_async_copy(out_ref, out_ref, out_sem).wait()


def by_head(query_rows, key_rows, value_rows, window_offsets):
    shape = query_rows.shape
    devices = lax.axis_size("slab") * lax.axis_size("strip")
    layers = devices // (FT * BY)
    tiles = layers * ROW_TILES * COL_TILES
    windows = window_offsets.shape[0]
    tokens, width = shape[0] * shape[1], shape[2]
    flat = [x.reshape(tokens, width) for x in (query_rows, key_rows, value_rows)]
    pairs = tiles * windows * TOKENS * TOKENS
    out = pl.pallas_call(
        functools.partial(head_kernel, layers, windows),
        out_shape=jax.ShapeDtypeStruct((tokens, width), jnp.bfloat16),
        in_specs=[pl.BlockSpec(memory_space=pltpu.SMEM)]
        + [pl.BlockSpec(memory_space=pl.ANY)] * 3,
        out_specs=pl.BlockSpec(memory_space=pl.ANY),
        scratch_shapes=[
            pltpu.VMEM((devices, 2, tokens, HD), jnp.bfloat16),
            pltpu.VMEM((layers * BY, FT, tokens, HD), jnp.bfloat16),
            pltpu.VMEM((layers * BY, FT, tokens, HD), jnp.bfloat16),
            pltpu.VMEM((tiles, FT, 64, HD), jnp.bfloat16),
            pltpu.VMEM((tiles + 1, FT, 64, 2 * HD), jnp.bfloat16),
            pltpu.VMEM((FT, TILE_H, COLS, TILE_W, HD), jnp.float32),
            pltpu.VMEM((FT, TILE_H, COLS, TILE_W, HD), jnp.float32),
            pltpu.SemaphoreType.DMA((devices,)),
            pltpu.SemaphoreType.DMA((layers * BY,)),
            pltpu.SemaphoreType.DMA,
            pltpu.SemaphoreType.DMA,
            pltpu.SemaphoreType.DMA,
            pltpu.SemaphoreType.DMA,
        ],
        compiler_params=pltpu.CompilerParams(
            collective_id=0, has_side_effects=True, vmem_limit_bytes=60 * 2**20
        ),
        cost_estimate=pl.CostEstimate(
            flops=6 * pairs * HD, bytes_accessed=8 * tokens * width, transcendentals=pairs
        ),
    )(window_offsets.T, *flat)
    return out.reshape(shape)


def solution(mesh):
    specs = P("slab", "strip", None)

    def attention(query_rows, key_rows, value_rows, window_offsets):
        slabs, strips = mesh.shape["slab"], mesh.shape["strip"]
        lines, width, features = query_rows.shape
        fits = slabs * strips * HD == features and lines == slabs * TILE_H
        fits = fits and strips == 2 and width == strips * COLS * TILE_W and slabs % 8 == 0
        return jax.shard_map(
            by_head if fits else per_device,
            mesh=mesh,
            in_specs=(specs, specs, specs, P()),
            out_specs=specs,
            check_vma=False,
        )(query_rows, key_rows, value_rows, window_offsets)

    return attention
```

```python
import functools
import math

import jax
import jax.numpy as jnp
from jax import lax
from jax.experimental import pallas as pl
from jax.experimental.pallas import tpu as pltpu
from jax.sharding import PartitionSpec as P

HD = 128
TILE_T = 4
TILE_H = 8
TILE_W = 8


def swapped(value, axis, apart):
    mask = 2**apart
    pairs = [(source, source ^ mask) for source in range(lax.axis_size(axis))]
    return lax.ppermute(value, axis, pairs)


def from_behind(block, axis, distance):
    devices = range(lax.axis_size(axis))
    route = [(i - distance, i) for i in devices if i - distance in devices]
    return lax.ppermute(block, axis, route)


def pair_transpose(pieces, move_piece, bit_order):
    slab_pos = lax.axis_index("slab")
    shaped = pieces.reshape((2, 2, 2) + pieces.shape[1:])
    for bit_num in bit_order:
        axis_num = 2 - bit_num
        is_upper = slab_pos >> bit_num & 1 == 1
        lower_half = jnp.take(shaped, 0, axis=axis_num)
        upper_half = jnp.take(shaped, 1, axis=axis_num)
        kept_part = jnp.where(is_upper, upper_half, lower_half)
        sent_part = jnp.where(is_upper, lower_half, upper_half)
        got_part = move_piece(sent_part, bit_num)
        shaped = jnp.stack(
            [jnp.where(is_upper, got_part, kept_part), jnp.where(is_upper, kept_part, got_part)],
            axis=axis_num,
        )
    return shaped.reshape((8,) + shaped.shape[3:])


def widen_rims(own_cols, rim_cols, right_side):
    blank = jnp.zeros_like(rim_cols)
    return jnp.concatenate(
        [jnp.where(right_side, blank, rim_cols), own_cols, jnp.where(right_side, rim_cols, blank)],
        axis=-2,
    )


def send_tiles(segment, bit_num):
    return swapped(segment, "slab", bit_num)


def send_rows(segment, bit_num):
    return swapped(segment, "slab", bit_num)


def per_device(query_rows, key_rows, value_rows, window_offsets):
    bit_order = (0, 1, 2)
    line_count = query_rows.shape[0]
    stacked = jnp.stack([query_rows, key_rows, value_rows])
    by_head = lax.all_to_all(stacked, "strip", split_axis=3, concat_axis=2, tiled=True)
    full_width = by_head.shape[2]
    half_width = full_width // 2
    piece_width = by_head.shape[3] // 4
    device_heads = piece_width // HD
    pieces = by_head.reshape(3, line_count, 2, half_width, 4, piece_width).transpose(
        2, 4, 0, 1, 3, 5
    )
    pieces = pieces.reshape(8, 3, line_count, half_width, piece_width)
    arrived = pair_transpose(pieces, send_tiles, bit_order)
    tile_block = arrived.reshape(TILE_T, 2, 3, line_count, half_width, piece_width).transpose(
        2, 0, 1, 3, 4, 5
    )
    tile_block = tile_block.reshape(3, TILE_T, 2 * line_count, half_width, piece_width)
    query_block = tile_block[0]
    key_value = tile_block[1:]
    slab_pos = lax.axis_index("slab")
    frame_tile = slab_pos // 8
    side_half = slab_pos // 4 % 2
    right_side = side_half == 0
    edge_cols = jnp.where(
        right_side, key_value[..., half_width - TILE_W :, :], key_value[..., :TILE_W, :]
    )
    rim_cols = swapped(edge_cols, "slab", 2)
    carried = jnp.concatenate([key_value, rim_cols], axis=-2)
    earlier_layer = from_behind(carried, "slab", 8)
    later_layer = from_behind(carried, "slab", -8)
    extended = jnp.stack(
        [
            widen_rims(layer_data[..., :half_width, :], layer_data[..., half_width:, :], right_side)
            for layer_data in (earlier_layer, carried, later_layer)
        ]
    )
    tile_rows = 2 * line_count // TILE_H
    tile_cols = half_width // TILE_W
    wide_cols = tile_cols + 2
    tokens = TILE_T * TILE_H * TILE_W
    key_tiles = extended.reshape(
        3, 2, TILE_T, tile_rows, TILE_H, wide_cols, TILE_W, device_heads, HD
    )
    key_tiles = key_tiles.transpose(0, 3, 5, 1, 2, 4, 6, 7, 8).reshape(
        3 * tile_rows * wide_cols, 2, tokens, device_heads, HD
    )
    query_tiles = query_block.reshape(
        TILE_T, tile_rows, TILE_H, tile_cols, TILE_W, device_heads, HD
    )
    query_tiles = query_tiles.transpose(1, 3, 0, 2, 4, 5, 6).reshape(
        tile_rows * tile_cols, tokens, device_heads, HD
    )
    query_count = tile_rows * tile_cols
    window_count = window_offsets.shape[0]
    tile_ids = jnp.arange(query_count, dtype=jnp.int32)
    row_tile = (tile_ids // tile_cols)[:, None]
    col_local = (tile_ids % tile_cols)[:, None]
    shift_frame = window_offsets[:, 0][None, :]
    shift_row = window_offsets[:, 1][None, :]
    shift_col = window_offsets[:, 2][None, :]
    key_frame = frame_tile + shift_frame
    key_row = row_tile + shift_row
    key_col = side_half * tile_cols + col_local + shift_col
    frame_total = lax.axis_size("slab") // 8
    inside = (key_frame >= 0) & (key_frame < frame_total) & (key_row >= 0) & (key_row < tile_rows)
    inside = inside & (key_col >= 0) & (key_col < 2 * tile_cols)
    flat_index = (
        (1 + shift_frame) * (tile_rows * wide_cols)
        + jnp.clip(key_row, 0, tile_rows - 1) * wide_cols
        + 1
        + col_local
        + shift_col
    )
    tiles_step = min(query_count, max(1, 512 // tokens))
    step_count = query_count // tiles_step
    score_scale = HD ** (-0.5)

    def attend(inputs):
        query_tile, tile_index, tile_live = inputs
        window_tiles = jnp.take(key_tiles, tile_index.reshape(-1), axis=0)
        window_tiles = window_tiles.reshape(tiles_step, window_count, 2, tokens, device_heads, HD)
        window_keys = window_tiles[:, :, 0].reshape(
            tiles_step, window_count * tokens, device_heads, HD
        )
        window_values = window_tiles[:, :, 1].reshape(
            tiles_step, window_count * tokens, device_heads, HD
        )
        scores = jnp.einsum(
            "pqhd,pkhd->phqk", query_tile, window_keys, preferred_element_type=jnp.float32
        )
        key_live = jnp.repeat(tile_live, tokens, axis=1)
        scores = jnp.where(key_live[:, None, None, :], scores, -1e30)
        row_max = jnp.max(scores, axis=-1, keepdims=True)
        raised = jnp.exp((scores - row_max) * score_scale)
        weights = (raised / jnp.sum(raised, axis=-1, keepdims=True)).astype(jnp.bfloat16)
        mixed_out = jnp.einsum(
            "phqk,pkhd->pqhd", weights, window_values, preferred_element_type=jnp.float32
        )
        return mixed_out.astype(jnp.bfloat16)

    attended = lax.map(
        attend,
        (
            query_tiles.reshape(step_count, tiles_step, tokens, device_heads, HD),
            flat_index.reshape(step_count, tiles_step, window_count),
            inside.reshape(step_count, tiles_step, window_count),
        ),
    )
    attended = attended.reshape(tile_rows, tile_cols, TILE_T, TILE_H, TILE_W, device_heads, HD)
    attended = attended.transpose(2, 0, 3, 1, 4, 5, 6).reshape(
        8, line_count, half_width, piece_width
    )
    returned = pair_transpose(attended, send_rows, bit_order)
    merged = returned.reshape(2, 4, line_count, half_width, piece_width).transpose(2, 0, 3, 1, 4)
    merged = merged.reshape(line_count, full_width, 4 * piece_width)
    return lax.all_to_all(merged, "strip", split_axis=1, concat_axis=2, tiled=True)


BY = 4
FT = TILE_T
COLS = 3
ROW_TILES = 2
COL_TILES = 6
TOKENS = TILE_T * TILE_H * TILE_W


def head_kernel(layers, windows, off_ref, q_ref, k_ref, v_ref, out_ref, kv_in, q_in, o_buf,
                k_tiles, v_tiles, q_wide, o_wide, kv_sems, q_sems, out_sem, kv_sent, q_sent,
                o_sent):
    devices = layers * FT * BY
    tiles = layers * ROW_TILES * COL_TILES
    me = lax.axis_index("slab") * 2 + lax.axis_index("strip")
    layer, frame, lane = me // (FT * BY), me // BY % FT, me % BY

    def mesh_id(device):
        return (device // 2, device % 2)

    def device_of(a, f, b):
        return (a * FT + f) * BY + b

    def columns(device):
        return pl.ds(pl.multiple_of(device * HD, HD), HD)

    barrier = pltpu.get_barrier_semaphore()

    @pl.loop(1, devices)
    def _(i):
        pl.semaphore_signal(
            barrier, inc=1, device_id=mesh_id((me + i) % devices),
            device_id_type=pl.DeviceIdType.MESH,
        )

    pl.semaphore_wait(barrier, devices - 1)

    def kv_step(i):
        return (layers - 1) - i % layers, i // layers % FT, i // (layers * FT)

    def group_step(n):
        return (layers - 1) - n // 2 % layers, n // (2 * layers) * 2 + n % 2

    def q_step(i):
        a, b = group_step(i // FT)
        return a, i % FT, b

    def ahead(step):
        a, f, b = step
        return device_of((layer + a) % layers, (frame + f) % FT, (lane + b) % BY)

    kv_self = layers - 1
    q_self = (layers - 1) * 2 * FT
    q_early = devices // 2
    my_group = layer * BY + lane

    pltpu.make_async_copy(k_ref.at[:, columns(me)], kv_in.at[me, 0], kv_sems.at[me]).start()
    pltpu.make_async_copy(v_ref.at[:, columns(me)], kv_in.at[me, 1], kv_sems.at[me]).start()
    pltpu.make_async_copy(
        q_ref.at[:, columns(me)], q_in.at[my_group, frame], q_sems.at[my_group]
    ).start()

    def send_kv(i):
        to = ahead(kv_step(i))
        for part, ref in enumerate((k_ref, v_ref)):
            pltpu.make_async_remote_copy(
                src_ref=ref.at[:, columns(to)],
                dst_ref=kv_in.at[me, part],
                send_sem=kv_sent,
                recv_sem=kv_sems.at[me],
                device_id=mesh_id(to),
                device_id_type=pl.DeviceIdType.MESH,
            ).start()

    def send_q(i):
        to = ahead(q_step(i))
        pltpu.make_async_remote_copy(
            src_ref=q_ref.at[:, columns(to)],
            dst_ref=q_in.at[my_group, frame],
            send_sem=q_sent,
            recv_sem=q_sems.at[my_group],
            device_id=mesh_id(to),
            device_id_type=pl.DeviceIdType.MESH,
        ).start()

    pl.loop(0, kv_self)(send_kv)
    pl.loop(kv_self + 1, devices)(send_kv)
    pl.loop(0, q_self)(send_q)
    pl.loop(q_self + 1, q_early)(send_q)

    @pl.loop(0, tiles)
    def _(t):
        v_tiles[t, :, :, HD:] = jnp.ones((FT, 64, HD), jnp.bfloat16)

    v_tiles[tiles] = jnp.zeros((FT, 64, 2 * HD), jnp.bfloat16)

    @pl.loop(0, devices)
    def _(i):
        @pl.when(i >= q_early)
        def _():
            send_q(i)

        a, f, b = kv_step(i)
        a, f, b = (layer + layers - a) % layers, (frame + FT - f) % FT, (lane + BY - b) % BY
        source = device_of(a, f, b)
        pltpu.make_async_copy(kv_in.at[source], kv_in.at[source], kv_sems.at[source]).wait()
        first = (a * ROW_TILES + b // 2) * COL_TILES + b % 2 * COLS
        key_block = kv_in[source, 0].astype(jnp.float32).reshape(TILE_H, COLS, TILE_W, HD)
        value_block = kv_in[source, 1].astype(jnp.float32).reshape(TILE_H, COLS, TILE_W, HD)
        for c in range(COLS):
            k_tiles[first + c, f] = key_block[:, c].reshape(64, HD).astype(jnp.bfloat16)
            v_tiles[first + c, f, :, :HD] = (
                value_block[:, c].reshape(64, HD).astype(jnp.bfloat16)
            )

    factor = HD ** (-0.5) * math.log2(math.e)

    @pl.loop(0, layers * BY)
    def _(n):
        a, b = group_step(n)
        a, b = (layer + layers - a) % layers, (lane + BY - b) % BY
        group = a * BY + b
        pltpu.make_async_copy(q_in.at[group], q_in.at[group], q_sems.at[group]).wait()
        q_wide[...] = q_in[group].astype(jnp.float32).reshape(FT, TILE_H, COLS, TILE_W, HD)

        @pl.loop(0, COLS)
        def _(c):
            row, col = b // 2, b % 2 * COLS + c
            own = (a * ROW_TILES + row) * COL_TILES + col
            query = q_wide[:, :, c].reshape(TOKENS, HD).astype(jnp.bfloat16)
            scores, picks = [], []
            for w in range(windows):
                ka, kr, kc = a + off_ref[0, w], row + off_ref[1, w], col + off_ref[2, w]
                live = (ka >= 0) & (ka < layers) & (kr >= 0) & (kr < ROW_TILES)
                live = live & (kc >= 0) & (kc < COL_TILES)
                tile = (ka * ROW_TILES + kr) * COL_TILES + kc
                picks.append(jnp.where(live, tile, tiles))
                keys = k_tiles[jnp.where(live, tile, own)].reshape(TOKENS, HD)
                scores.append(
                    lax.dot_general(
                        query, keys, (((1,), (1,)), ((), ())),
                        preferred_element_type=jnp.float32,
                    )
                )
            top = functools.reduce(jnp.maximum, scores)
            top = jnp.max(top, axis=-1, keepdims=True)
            total = jnp.zeros((TOKENS, 2 * HD), jnp.float32)
            for score, pick in zip(scores, picks):
                raised = jnp.exp2((score - top) * factor).astype(jnp.bfloat16)
                values = v_tiles[pick].reshape(TOKENS, 2 * HD)
                total += jnp.dot(raised, values, preferred_element_type=jnp.float32)
            mixed = total[:, :HD] / total[:, HD:]
            o_wide[:, :, c] = mixed.reshape(FT, TILE_H, TILE_W, HD)

        o_buf[group] = o_wide[...].reshape(FT, 192, HD).astype(jnp.bfloat16)

        @pl.loop(0, FT)
        def _(f):
            to = device_of(a, f, b)

            @pl.when(to == me)
            def _():
                pltpu.make_async_copy(
                    o_buf.at[group, f], out_ref.at[:, columns(me)], out_sem
                ).start()

            @pl.when(to != me)
            def _():
                pltpu.make_async_remote_copy(
                    src_ref=o_buf.at[group, f],
                    dst_ref=out_ref.at[:, columns(me)],
                    send_sem=o_sent,
                    recv_sem=out_sem,
                    device_id=mesh_id(to),
                    device_id_type=pl.DeviceIdType.MESH,
                ).start()

    others = pl.ds(0, devices - 1)
    pltpu.make_async_copy(kv_in.at[others], kv_in.at[others], kv_sent).wait()
    sent = kv_in.at[others, 0]
    pltpu.make_async_copy(sent, sent, q_sent).wait()
    pltpu.make_async_copy(sent, sent, o_sent).wait()
    pltpu.make_async_copy(out_ref, out_ref, out_sem).wait()


def by_head(query_rows, key_rows, value_rows, window_offsets):
    shape = query_rows.shape
    devices = lax.axis_size("slab") * lax.axis_size("strip")
    layers = devices // (FT * BY)
    tiles = layers * ROW_TILES * COL_TILES
    windows = window_offsets.shape[0]
    tokens, width = shape[0] * shape[1], shape[2]
    flat = [x.reshape(tokens, width) for x in (query_rows, key_rows, value_rows)]
    pairs = tiles * windows * TOKENS * TOKENS
    out = pl.pallas_call(
        functools.partial(head_kernel, layers, windows),
        out_shape=pltpu.VMEM((tokens, width), jnp.bfloat16),
        in_specs=[pl.BlockSpec(memory_space=pltpu.SMEM)]
        + [pl.BlockSpec(memory_space=pl.ANY)] * 3,
        out_specs=pl.BlockSpec(memory_space=pl.ANY),
        scratch_shapes=[
            pltpu.VMEM((devices, 2, tokens, HD), jnp.bfloat16),
            pltpu.VMEM((layers * BY, FT, tokens, HD), jnp.bfloat16),
            pltpu.VMEM((layers * BY, FT, tokens, HD), jnp.bfloat16),
            pltpu.VMEM((tiles, FT, 64, HD), jnp.bfloat16),
            pltpu.VMEM((tiles + 1, FT, 64, 2 * HD), jnp.bfloat16),
            pltpu.VMEM((FT, TILE_H, COLS, TILE_W, HD), jnp.float32),
            pltpu.VMEM((FT, TILE_H, COLS, TILE_W, HD), jnp.float32),
            pltpu.SemaphoreType.DMA((devices,)),
            pltpu.SemaphoreType.DMA((layers * BY,)),
            pltpu.SemaphoreType.DMA,
            pltpu.SemaphoreType.DMA,
            pltpu.SemaphoreType.DMA,
            pltpu.SemaphoreType.DMA,
        ],
        compiler_params=pltpu.CompilerParams(
            collective_id=0, has_side_effects=True, vmem_limit_bytes=60 * 2**20
        ),
        cost_estimate=pl.CostEstimate(
            flops=6 * pairs * HD, bytes_accessed=8 * tokens * width, transcendentals=pairs
        ),
    )(window_offsets.T, *flat)
    return out.reshape(shape)


def solution(mesh):
    specs = P("slab", "strip", None)

    def attention(query_rows, key_rows, value_rows, window_offsets):
        slabs, strips = mesh.shape["slab"], mesh.shape["strip"]
        lines, width, features = query_rows.shape
        fits = slabs * strips * HD == features and lines == slabs * TILE_H
        fits = fits and strips == 2 and width == strips * COLS * TILE_W and slabs % 8 == 0
        return jax.shard_map(
            by_head if fits else per_device,
            mesh=mesh,
            in_specs=(specs, specs, specs, P()),
            out_specs=specs,
            check_vma=False,
        )(query_rows, key_rows, value_rows, window_offsets)

    return attention
```

```python
import functools
import math

import jax
import jax.numpy as jnp
from jax import lax
from jax.experimental import pallas as pl
from jax.experimental.pallas import tpu as pltpu
from jax.sharding import PartitionSpec as P

HD = 128
TILE_T = 4
TILE_H = 8
TILE_W = 8


def swapped(value, axis, apart):
    mask = 2**apart
    pairs = [(source, source ^ mask) for source in range(lax.axis_size(axis))]
    return lax.ppermute(value, axis, pairs)


def from_behind(block, axis, distance):
    devices = range(lax.axis_size(axis))
    route = [(i - distance, i) for i in devices if i - distance in devices]
    return lax.ppermute(block, axis, route)


def pair_transpose(pieces, move_piece, bit_order):
    slab_pos = lax.axis_index("slab")
    shaped = pieces.reshape((2, 2, 2) + pieces.shape[1:])
    for bit_num in bit_order:
        axis_num = 2 - bit_num
        is_upper = slab_pos >> bit_num & 1 == 1
        lower_half = jnp.take(shaped, 0, axis=axis_num)
        upper_half = jnp.take(shaped, 1, axis=axis_num)
        kept_part = jnp.where(is_upper, upper_half, lower_half)
        sent_part = jnp.where(is_upper, lower_half, upper_half)
        got_part = move_piece(sent_part, bit_num)
        shaped = jnp.stack(
            [jnp.where(is_upper, got_part, kept_part), jnp.where(is_upper, kept_part, got_part)],
            axis=axis_num,
        )
    return shaped.reshape((8,) + shaped.shape[3:])


def widen_rims(own_cols, rim_cols, right_side):
    blank = jnp.zeros_like(rim_cols)
    return jnp.concatenate(
        [jnp.where(right_side, blank, rim_cols), own_cols, jnp.where(right_side, rim_cols, blank)],
        axis=-2,
    )


def send_tiles(segment, bit_num):
    return swapped(segment, "slab", bit_num)


def send_rows(segment, bit_num):
    return swapped(segment, "slab", bit_num)


def per_device(query_rows, key_rows, value_rows, window_offsets):
    bit_order = (0, 1, 2)
    line_count = query_rows.shape[0]
    stacked = jnp.stack([query_rows, key_rows, value_rows])
    by_head = lax.all_to_all(stacked, "strip", split_axis=3, concat_axis=2, tiled=True)
    full_width = by_head.shape[2]
    half_width = full_width // 2
    piece_width = by_head.shape[3] // 4
    device_heads = piece_width // HD
    pieces = by_head.reshape(3, line_count, 2, half_width, 4, piece_width).transpose(
        2, 4, 0, 1, 3, 5
    )
    pieces = pieces.reshape(8, 3, line_count, half_width, piece_width)
    arrived = pair_transpose(pieces, send_tiles, bit_order)
    tile_block = arrived.reshape(TILE_T, 2, 3, line_count, half_width, piece_width).transpose(
        2, 0, 1, 3, 4, 5
    )
    tile_block = tile_block.reshape(3, TILE_T, 2 * line_count, half_width, piece_width)
    query_block = tile_block[0]
    key_value = tile_block[1:]
    slab_pos = lax.axis_index("slab")
    frame_tile = slab_pos // 8
    side_half = slab_pos // 4 % 2
    right_side = side_half == 0
    edge_cols = jnp.where(
        right_side, key_value[..., half_width - TILE_W :, :], key_value[..., :TILE_W, :]
    )
    rim_cols = swapped(edge_cols, "slab", 2)
    carried = jnp.concatenate([key_value, rim_cols], axis=-2)
    earlier_layer = from_behind(carried, "slab", 8)
    later_layer = from_behind(carried, "slab", -8)
    extended = jnp.stack(
        [
            widen_rims(layer_data[..., :half_width, :], layer_data[..., half_width:, :], right_side)
            for layer_data in (earlier_layer, carried, later_layer)
        ]
    )
    tile_rows = 2 * line_count // TILE_H
    tile_cols = half_width // TILE_W
    wide_cols = tile_cols + 2
    tokens = TILE_T * TILE_H * TILE_W
    key_tiles = extended.reshape(
        3, 2, TILE_T, tile_rows, TILE_H, wide_cols, TILE_W, device_heads, HD
    )
    key_tiles = key_tiles.transpose(0, 3, 5, 1, 2, 4, 6, 7, 8).reshape(
        3 * tile_rows * wide_cols, 2, tokens, device_heads, HD
    )
    query_tiles = query_block.reshape(
        TILE_T, tile_rows, TILE_H, tile_cols, TILE_W, device_heads, HD
    )
    query_tiles = query_tiles.transpose(1, 3, 0, 2, 4, 5, 6).reshape(
        tile_rows * tile_cols, tokens, device_heads, HD
    )
    query_count = tile_rows * tile_cols
    window_count = window_offsets.shape[0]
    tile_ids = jnp.arange(query_count, dtype=jnp.int32)
    row_tile = (tile_ids // tile_cols)[:, None]
    col_local = (tile_ids % tile_cols)[:, None]
    shift_frame = window_offsets[:, 0][None, :]
    shift_row = window_offsets[:, 1][None, :]
    shift_col = window_offsets[:, 2][None, :]
    key_frame = frame_tile + shift_frame
    key_row = row_tile + shift_row
    key_col = side_half * tile_cols + col_local + shift_col
    frame_total = lax.axis_size("slab") // 8
    inside = (key_frame >= 0) & (key_frame < frame_total) & (key_row >= 0) & (key_row < tile_rows)
    inside = inside & (key_col >= 0) & (key_col < 2 * tile_cols)
    flat_index = (
        (1 + shift_frame) * (tile_rows * wide_cols)
        + jnp.clip(key_row, 0, tile_rows - 1) * wide_cols
        + 1
        + col_local
        + shift_col
    )
    tiles_step = min(query_count, max(1, 512 // tokens))
    step_count = query_count // tiles_step
    score_scale = HD ** (-0.5)

    def attend(inputs):
        query_tile, tile_index, tile_live = inputs
        window_tiles = jnp.take(key_tiles, tile_index.reshape(-1), axis=0)
        window_tiles = window_tiles.reshape(tiles_step, window_count, 2, tokens, device_heads, HD)
        window_keys = window_tiles[:, :, 0].reshape(
            tiles_step, window_count * tokens, device_heads, HD
        )
        window_values = window_tiles[:, :, 1].reshape(
            tiles_step, window_count * tokens, device_heads, HD
        )
        scores = jnp.einsum(
            "pqhd,pkhd->phqk", query_tile, window_keys, preferred_element_type=jnp.float32
        )
        key_live = jnp.repeat(tile_live, tokens, axis=1)
        scores = jnp.where(key_live[:, None, None, :], scores, -1e30)
        row_max = jnp.max(scores, axis=-1, keepdims=True)
        raised = jnp.exp((scores - row_max) * score_scale)
        weights = (raised / jnp.sum(raised, axis=-1, keepdims=True)).astype(jnp.bfloat16)
        mixed_out = jnp.einsum(
            "phqk,pkhd->pqhd", weights, window_values, preferred_element_type=jnp.float32
        )
        return mixed_out.astype(jnp.bfloat16)

    attended = lax.map(
        attend,
        (
            query_tiles.reshape(step_count, tiles_step, tokens, device_heads, HD),
            flat_index.reshape(step_count, tiles_step, window_count),
            inside.reshape(step_count, tiles_step, window_count),
        ),
    )
    attended = attended.reshape(tile_rows, tile_cols, TILE_T, TILE_H, TILE_W, device_heads, HD)
    attended = attended.transpose(2, 0, 3, 1, 4, 5, 6).reshape(
        8, line_count, half_width, piece_width
    )
    returned = pair_transpose(attended, send_rows, bit_order)
    merged = returned.reshape(2, 4, line_count, half_width, piece_width).transpose(2, 0, 3, 1, 4)
    merged = merged.reshape(line_count, full_width, 4 * piece_width)
    return lax.all_to_all(merged, "strip", split_axis=1, concat_axis=2, tiled=True)


BY = 4
FT = TILE_T
COLS = 3
ROW_TILES = 2
COL_TILES = 6
TOKENS = TILE_T * TILE_H * TILE_W


def head_kernel(layers, windows, off_ref, q_ref, k_ref, v_ref, out_ref, kv_in, q_in, o_buf,
                k_tiles, v_tiles, q_wide, o_wide, kv_sems, q_sems, out_sem, kv_sent, q_sent,
                o_sent):
    devices = layers * FT * BY
    tiles = layers * ROW_TILES * COL_TILES
    me = lax.axis_index("slab") * 2 + lax.axis_index("strip")
    layer, frame, lane = me // (FT * BY), me // BY % FT, me % BY

    def mesh_id(device):
        return (lax.div(device, 2), lax.rem(device, 2))

    def device_of(a, f, b):
        return (a * FT + f) * BY + b

    def columns(device):
        return pl.ds(pl.multiple_of(device * HD, HD), HD)

    barrier = pltpu.get_barrier_semaphore()

    @pl.loop(1, devices)
    def _(i):
        pl.semaphore_signal(
            barrier, inc=1, device_id=mesh_id(lax.rem(me + i, devices)),
            device_id_type=pl.DeviceIdType.MESH,
        )

    my_group = layer * BY + lane

    pltpu.make_async_copy(k_ref.at[:, columns(me)], kv_in.at[me, 0], kv_sems.at[me]).start()
    pltpu.make_async_copy(v_ref.at[:, columns(me)], kv_in.at[me, 1], kv_sems.at[me]).start()
    pltpu.make_async_copy(
        q_ref.at[:, columns(me)], q_in.at[my_group, frame], q_sems.at[my_group]
    ).start()

    @pl.loop(0, tiles)
    def _(t):
        v_tiles[t, :, :, HD:] = jnp.ones((FT, 64, HD), jnp.bfloat16)

    v_tiles[tiles] = jnp.zeros((FT, 64, 2 * HD), jnp.bfloat16)

    pl.semaphore_wait(barrier, devices - 1)

    def kv_step(i):
        return (layers - 1) - i % layers, i // layers % FT, i // (layers * FT)

    def group_step(n):
        return (layers - 1) - n // 2 % layers, n // (2 * layers) * 2 + n % 2

    def q_step(i):
        a, b = group_step(i // FT)
        return a, i % FT, b

    def ahead(step):
        a, f, b = step
        return device_of((layer + a) % layers, (frame + f) % FT, (lane + b) % BY)

    kv_self = layers - 1
    q_self = (layers - 1) * 2 * FT
    q_early = devices // 2
    def send_kv(i):
        to = ahead(kv_step(i))
        for part, ref in enumerate((k_ref, v_ref)):
            pltpu.make_async_remote_copy(
                src_ref=ref.at[:, columns(to)],
                dst_ref=kv_in.at[me, part],
                send_sem=kv_sent,
                recv_sem=kv_sems.at[me],
                device_id=mesh_id(to),
                device_id_type=pl.DeviceIdType.MESH,
            ).start()

    def send_q(i):
        to = ahead(q_step(i))
        pltpu.make_async_remote_copy(
            src_ref=q_ref.at[:, columns(to)],
            dst_ref=q_in.at[my_group, frame],
            send_sem=q_sent,
            recv_sem=q_sems.at[my_group],
            device_id=mesh_id(to),
            device_id_type=pl.DeviceIdType.MESH,
        ).start()

    pl.loop(0, kv_self)(send_kv)
    pl.loop(kv_self + 1, devices)(send_kv)
    pl.loop(0, q_self)(send_q)
    pl.loop(q_self + 1, q_early)(send_q)

    @pl.loop(0, devices)
    def _(i):
        @pl.when(i >= q_early)
        def _():
            send_q(i)

        a, f, b = kv_step(i)
        a, f, b = (layer + layers - a) % layers, (frame + FT - f) % FT, (lane + BY - b) % BY
        source = device_of(a, f, b)
        pltpu.make_async_copy(kv_in.at[source], kv_in.at[source], kv_sems.at[source]).wait()
        first = (a * ROW_TILES + b // 2) * COL_TILES + b % 2 * COLS
        key_block = kv_in[source, 0].astype(jnp.float32).reshape(TILE_H, COLS, TILE_W, HD)
        value_block = kv_in[source, 1].astype(jnp.float32).reshape(TILE_H, COLS, TILE_W, HD)
        for c in range(COLS):
            k_tiles[first + c, f] = key_block[:, c].reshape(64, HD).astype(jnp.bfloat16)
            v_tiles[first + c, f, :, :HD] = (
                value_block[:, c].reshape(64, HD).astype(jnp.bfloat16)
            )

    factor = HD ** (-0.5) * math.log2(math.e)

    @pl.loop(0, layers * BY)
    def _(n):
        a, b = group_step(n)
        a, b = (layer + layers - a) % layers, (lane + BY - b) % BY
        group = a * BY + b
        pltpu.make_async_copy(q_in.at[group], q_in.at[group], q_sems.at[group]).wait()
        q_wide[...] = q_in[group].astype(jnp.float32).reshape(FT, TILE_H, COLS, TILE_W, HD)

        @pl.loop(0, COLS)
        def _(c):
            row, col = b // 2, b % 2 * COLS + c
            own = (a * ROW_TILES + row) * COL_TILES + col
            query = q_wide[:, :, c].reshape(TOKENS, HD).astype(jnp.bfloat16)
            scores, picks = [], []
            for w in range(windows):
                ka, kr, kc = a + off_ref[0, w], row + off_ref[1, w], col + off_ref[2, w]
                live = (ka >= 0) & (ka < layers) & (kr >= 0) & (kr < ROW_TILES)
                live = live & (kc >= 0) & (kc < COL_TILES)
                tile = (ka * ROW_TILES + kr) * COL_TILES + kc
                picks.append(jnp.where(live, tile, tiles))
                keys = k_tiles[jnp.where(live, tile, own)].reshape(TOKENS, HD)
                scores.append(
                    lax.dot_general(
                        query, keys, (((1,), (1,)), ((), ())),
                        preferred_element_type=jnp.float32,
                    )
                )
            top = functools.reduce(jnp.maximum, scores)
            top = jnp.max(top, axis=-1, keepdims=True)
            total = jnp.zeros((TOKENS, 2 * HD), jnp.float32)
            for score, pick in zip(scores, picks):
                raised = jnp.exp2((score - top) * factor).astype(jnp.bfloat16)
                values = v_tiles[pick].reshape(TOKENS, 2 * HD)
                total += jnp.dot(raised, values, preferred_element_type=jnp.float32)
            mixed = total[:, :HD] / total[:, HD:]
            o_wide[:, :, c] = mixed.reshape(FT, TILE_H, TILE_W, HD)

        o_buf[group] = o_wide[...].reshape(FT, 192, HD).astype(jnp.bfloat16)

        @pl.loop(0, FT)
        def _(turn):
            f = lax.rem(frame + turn, FT)
            to = device_of(a, f, b)

            @pl.when(to == me)
            def _():
                pltpu.make_async_copy(
                    o_buf.at[group, f], out_ref.at[:, columns(me)], out_sem
                ).start()

            @pl.when(to != me)
            def _():
                pltpu.make_async_remote_copy(
                    src_ref=o_buf.at[group, f],
                    dst_ref=out_ref.at[:, columns(me)],
                    send_sem=o_sent,
                    recv_sem=out_sem,
                    device_id=mesh_id(to),
                    device_id_type=pl.DeviceIdType.MESH,
                ).start()

    others = pl.ds(0, devices - 1)
    pltpu.make_async_copy(kv_in.at[others], kv_in.at[others], kv_sent).wait()
    sent = kv_in.at[others, 0]
    pltpu.make_async_copy(sent, sent, q_sent).wait()
    pltpu.make_async_copy(sent, sent, o_sent).wait()
    pltpu.make_async_copy(out_ref, out_ref, out_sem).wait()


def by_head(query_rows, key_rows, value_rows, window_offsets):
    shape = query_rows.shape
    devices = lax.axis_size("slab") * lax.axis_size("strip")
    layers = devices // (FT * BY)
    tiles = layers * ROW_TILES * COL_TILES
    windows = window_offsets.shape[0]
    tokens, width = shape[0] * shape[1], shape[2]
    flat = [x.reshape(tokens, width) for x in (query_rows, key_rows, value_rows)]
    pairs = tiles * windows * TOKENS * TOKENS
    out = pl.pallas_call(
        functools.partial(head_kernel, layers, windows),
        out_shape=pltpu.VMEM((tokens, width), jnp.bfloat16),
        in_specs=[pl.BlockSpec(memory_space=pltpu.SMEM)]
        + [pl.BlockSpec(memory_space=pl.ANY)] * 3,
        out_specs=pl.BlockSpec(memory_space=pl.ANY),
        scratch_shapes=[
            pltpu.VMEM((devices, 2, tokens, HD), jnp.bfloat16),
            pltpu.VMEM((layers * BY, FT, tokens, HD), jnp.bfloat16),
            pltpu.VMEM((layers * BY, FT, tokens, HD), jnp.bfloat16),
            pltpu.VMEM((tiles, FT, 64, HD), jnp.bfloat16),
            pltpu.VMEM((tiles + 1, FT, 64, 2 * HD), jnp.bfloat16),
            pltpu.VMEM((FT, TILE_H, COLS, TILE_W, HD), jnp.float32),
            pltpu.VMEM((FT, TILE_H, COLS, TILE_W, HD), jnp.float32),
            pltpu.SemaphoreType.DMA((devices,)),
            pltpu.SemaphoreType.DMA((layers * BY,)),
            pltpu.SemaphoreType.DMA,
            pltpu.SemaphoreType.DMA,
            pltpu.SemaphoreType.DMA,
            pltpu.SemaphoreType.DMA,
        ],
        compiler_params=pltpu.CompilerParams(
            collective_id=0, has_side_effects=True, vmem_limit_bytes=60 * 2**20
        ),
        cost_estimate=pl.CostEstimate(
            flops=6 * pairs * HD, bytes_accessed=8 * tokens * width, transcendentals=pairs
        ),
    )(window_offsets.T, *flat)
    return out.reshape(shape)


def solution(mesh):
    specs = P("slab", "strip", None)

    def attention(query_rows, key_rows, value_rows, window_offsets):
        slabs, strips = mesh.shape["slab"], mesh.shape["strip"]
        lines, width, features = query_rows.shape
        fits = slabs * strips * HD == features and lines == slabs * TILE_H
        fits = fits and strips == 2 and width == strips * COLS * TILE_W and slabs % 8 == 0
        return jax.shard_map(
            by_head if fits else per_device,
            mesh=mesh,
            in_specs=(specs, specs, specs, P()),
            out_specs=specs,
            check_vma=False,
        )(query_rows, key_rows, value_rows, window_offsets)

    return attention
```

```python
import functools
import math

import jax
import jax.numpy as jnp
from jax import lax
from jax.experimental import pallas as pl
from jax.experimental.pallas import tpu as pltpu
from jax.sharding import PartitionSpec as P

HD = 128
TILE_T = 4
TILE_H = 8
TILE_W = 8


def swapped(value, axis, apart):
    mask = 2**apart
    pairs = [(source, source ^ mask) for source in range(lax.axis_size(axis))]
    return lax.ppermute(value, axis, pairs)


def from_behind(block, axis, distance):
    devices = range(lax.axis_size(axis))
    route = [(i - distance, i) for i in devices if i - distance in devices]
    return lax.ppermute(block, axis, route)


def pair_transpose(pieces, move_piece, bit_order):
    slab_pos = lax.axis_index("slab")
    shaped = pieces.reshape((2, 2, 2) + pieces.shape[1:])
    for bit_num in bit_order:
        axis_num = 2 - bit_num
        is_upper = slab_pos >> bit_num & 1 == 1
        lower_half = jnp.take(shaped, 0, axis=axis_num)
        upper_half = jnp.take(shaped, 1, axis=axis_num)
        kept_part = jnp.where(is_upper, upper_half, lower_half)
        sent_part = jnp.where(is_upper, lower_half, upper_half)
        got_part = move_piece(sent_part, bit_num)
        shaped = jnp.stack(
            [jnp.where(is_upper, got_part, kept_part), jnp.where(is_upper, kept_part, got_part)],
            axis=axis_num,
        )
    return shaped.reshape((8,) + shaped.shape[3:])


def widen_rims(own_cols, rim_cols, right_side):
    blank = jnp.zeros_like(rim_cols)
    return jnp.concatenate(
        [jnp.where(right_side, blank, rim_cols), own_cols, jnp.where(right_side, rim_cols, blank)],
        axis=-2,
    )


def send_tiles(segment, bit_num):
    return swapped(segment, "slab", bit_num)


def send_rows(segment, bit_num):
    return swapped(segment, "slab", bit_num)


def per_device(query_rows, key_rows, value_rows, window_offsets):
    bit_order = (0, 1, 2)
    line_count = query_rows.shape[0]
    stacked = jnp.stack([query_rows, key_rows, value_rows])
    by_head = lax.all_to_all(stacked, "strip", split_axis=3, concat_axis=2, tiled=True)
    full_width = by_head.shape[2]
    half_width = full_width // 2
    piece_width = by_head.shape[3] // 4
    device_heads = piece_width // HD
    pieces = by_head.reshape(3, line_count, 2, half_width, 4, piece_width).transpose(
        2, 4, 0, 1, 3, 5
    )
    pieces = pieces.reshape(8, 3, line_count, half_width, piece_width)
    arrived = pair_transpose(pieces, send_tiles, bit_order)
    tile_block = arrived.reshape(TILE_T, 2, 3, line_count, half_width, piece_width).transpose(
        2, 0, 1, 3, 4, 5
    )
    tile_block = tile_block.reshape(3, TILE_T, 2 * line_count, half_width, piece_width)
    query_block = tile_block[0]
    key_value = tile_block[1:]
    slab_pos = lax.axis_index("slab")
    frame_tile = slab_pos // 8
    side_half = slab_pos // 4 % 2
    right_side = side_half == 0
    edge_cols = jnp.where(
        right_side, key_value[..., half_width - TILE_W :, :], key_value[..., :TILE_W, :]
    )
    rim_cols = swapped(edge_cols, "slab", 2)
    carried = jnp.concatenate([key_value, rim_cols], axis=-2)
    earlier_layer = from_behind(carried, "slab", 8)
    later_layer = from_behind(carried, "slab", -8)
    extended = jnp.stack(
        [
            widen_rims(layer_data[..., :half_width, :], layer_data[..., half_width:, :], right_side)
            for layer_data in (earlier_layer, carried, later_layer)
        ]
    )
    tile_rows = 2 * line_count // TILE_H
    tile_cols = half_width // TILE_W
    wide_cols = tile_cols + 2
    tokens = TILE_T * TILE_H * TILE_W
    key_tiles = extended.reshape(
        3, 2, TILE_T, tile_rows, TILE_H, wide_cols, TILE_W, device_heads, HD
    )
    key_tiles = key_tiles.transpose(0, 3, 5, 1, 2, 4, 6, 7, 8).reshape(
        3 * tile_rows * wide_cols, 2, tokens, device_heads, HD
    )
    query_tiles = query_block.reshape(
        TILE_T, tile_rows, TILE_H, tile_cols, TILE_W, device_heads, HD
    )
    query_tiles = query_tiles.transpose(1, 3, 0, 2, 4, 5, 6).reshape(
        tile_rows * tile_cols, tokens, device_heads, HD
    )
    query_count = tile_rows * tile_cols
    window_count = window_offsets.shape[0]
    tile_ids = jnp.arange(query_count, dtype=jnp.int32)
    row_tile = (tile_ids // tile_cols)[:, None]
    col_local = (tile_ids % tile_cols)[:, None]
    shift_frame = window_offsets[:, 0][None, :]
    shift_row = window_offsets[:, 1][None, :]
    shift_col = window_offsets[:, 2][None, :]
    key_frame = frame_tile + shift_frame
    key_row = row_tile + shift_row
    key_col = side_half * tile_cols + col_local + shift_col
    frame_total = lax.axis_size("slab") // 8
    inside = (key_frame >= 0) & (key_frame < frame_total) & (key_row >= 0) & (key_row < tile_rows)
    inside = inside & (key_col >= 0) & (key_col < 2 * tile_cols)
    flat_index = (
        (1 + shift_frame) * (tile_rows * wide_cols)
        + jnp.clip(key_row, 0, tile_rows - 1) * wide_cols
        + 1
        + col_local
        + shift_col
    )
    tiles_step = min(query_count, max(1, 512 // tokens))
    step_count = query_count // tiles_step
    score_scale = HD ** (-0.5)

    def attend(inputs):
        query_tile, tile_index, tile_live = inputs
        window_tiles = jnp.take(key_tiles, tile_index.reshape(-1), axis=0)
        window_tiles = window_tiles.reshape(tiles_step, window_count, 2, tokens, device_heads, HD)
        window_keys = window_tiles[:, :, 0].reshape(
            tiles_step, window_count * tokens, device_heads, HD
        )
        window_values = window_tiles[:, :, 1].reshape(
            tiles_step, window_count * tokens, device_heads, HD
        )
        scores = jnp.einsum(
            "pqhd,pkhd->phqk", query_tile, window_keys, preferred_element_type=jnp.float32
        )
        key_live = jnp.repeat(tile_live, tokens, axis=1)
        scores = jnp.where(key_live[:, None, None, :], scores, -1e30)
        row_max = jnp.max(scores, axis=-1, keepdims=True)
        raised = jnp.exp((scores - row_max) * score_scale)
        weights = (raised / jnp.sum(raised, axis=-1, keepdims=True)).astype(jnp.bfloat16)
        mixed_out = jnp.einsum(
            "phqk,pkhd->pqhd", weights, window_values, preferred_element_type=jnp.float32
        )
        return mixed_out.astype(jnp.bfloat16)

    attended = lax.map(
        attend,
        (
            query_tiles.reshape(step_count, tiles_step, tokens, device_heads, HD),
            flat_index.reshape(step_count, tiles_step, window_count),
            inside.reshape(step_count, tiles_step, window_count),
        ),
    )
    attended = attended.reshape(tile_rows, tile_cols, TILE_T, TILE_H, TILE_W, device_heads, HD)
    attended = attended.transpose(2, 0, 3, 1, 4, 5, 6).reshape(
        8, line_count, half_width, piece_width
    )
    returned = pair_transpose(attended, send_rows, bit_order)
    merged = returned.reshape(2, 4, line_count, half_width, piece_width).transpose(2, 0, 3, 1, 4)
    merged = merged.reshape(line_count, full_width, 4 * piece_width)
    return lax.all_to_all(merged, "strip", split_axis=1, concat_axis=2, tiled=True)


BY = 4
FT = TILE_T
COLS = 3
ROW_TILES = 2
COL_TILES = 6
TOKENS = TILE_T * TILE_H * TILE_W


def head_kernel(layers, windows, off_ref, q_ref, k_ref, v_ref, out_ref, kv_in, q_in, o_buf,
                k_tiles, v_tiles, q_wide, o_wide, kv_sems, q_sems, out_sem, kv_sent, q_sent,
                o_sent):
    devices = layers * FT * BY
    tiles = layers * ROW_TILES * COL_TILES
    me = lax.axis_index("slab") * 2 + lax.axis_index("strip")
    layer, frame, lane = me // (FT * BY), me // BY % FT, me % BY

    def mesh_id(device):
        return (device // 2, device % 2)

    def device_of(a, f, b):
        return (a * FT + f) * BY + b

    def columns(device):
        return pl.ds(pl.multiple_of(device * HD, HD), HD)

    barrier = pltpu.get_barrier_semaphore()

    @pl.loop(1, devices)
    def _(i):
        pl.semaphore_signal(
            barrier, inc=1, device_id=mesh_id((me + i) % devices),
            device_id_type=pl.DeviceIdType.MESH,
        )

    pl.semaphore_wait(barrier, devices - 1)

    def kv_step(i):
        return (layers - 1) - i // (FT * BY), i % FT, i // FT % BY

    def group_step(n):
        return (layers - 1) - n // 2 % layers, n // (2 * layers) * 2 + n % 2

    def q_step(i):
        a, b = group_step(i // FT)
        return a, i % FT, b

    def ahead(step):
        a, f, b = step
        return device_of((layer + a) % layers, (frame + f) % FT, (lane + b) % BY)

    kv_self = (layers - 1) * FT * BY
    lead = FT * BY // 2
    q_self = (layers - 1) * 2 * FT
    q_early = devices // 2
    my_group = layer * BY + lane

    pltpu.make_async_copy(k_ref.at[:, columns(me)], kv_in.at[me, 0], kv_sems.at[me]).start()
    pltpu.make_async_copy(v_ref.at[:, columns(me)], kv_in.at[me, 1], kv_sems.at[me]).start()
    pltpu.make_async_copy(
        q_ref.at[:, columns(me)], q_in.at[my_group, frame], q_sems.at[my_group]
    ).start()

    def send_kv(i):
        to = ahead(kv_step(i))
        for part, ref in enumerate((k_ref, v_ref)):
            pltpu.make_async_remote_copy(
                src_ref=ref.at[:, columns(to)],
                dst_ref=kv_in.at[me, part],
                send_sem=kv_sent,
                recv_sem=kv_sems.at[me],
                device_id=mesh_id(to),
                device_id_type=pl.DeviceIdType.MESH,
            ).start()

    def send_q(i):
        to = ahead(q_step(i))
        pltpu.make_async_remote_copy(
            src_ref=q_ref.at[:, columns(to)],
            dst_ref=q_in.at[my_group, frame],
            send_sem=q_sent,
            recv_sem=q_sems.at[my_group],
            device_id=mesh_id(to),
            device_id_type=pl.DeviceIdType.MESH,
        ).start()

    @pl.loop(0, kv_self + lead)
    def _(j):
        pl.when(j < kv_self)(lambda: send_kv(j))
        near = kv_self + j - (kv_self + lead - FT * BY)
        pl.when(near > kv_self)(lambda: send_kv(near))

        @pl.when(j >= kv_self)
        def _():
            for k in range(q_early // lead):
                query = (j - kv_self) * (q_early // lead) + k
                pl.when(query != q_self)(lambda query=query: send_q(query))

    @pl.loop(0, tiles)
    def _(t):
        v_tiles[t, :, :, HD:] = jnp.ones((FT, 64, HD), jnp.bfloat16)

    v_tiles[tiles] = jnp.zeros((FT, 64, 2 * HD), jnp.bfloat16)

    @pl.loop(0, devices)
    def _(i):
        @pl.when((i >= lead) & (i < lead + devices - q_early))
        def _():
            send_q(i - lead + q_early)

        a, f, b = kv_step(i)
        a, f, b = (layer + layers - a) % layers, (frame + FT - f) % FT, (lane + BY - b) % BY
        source = device_of(a, f, b)
        pltpu.make_async_copy(kv_in.at[source], kv_in.at[source], kv_sems.at[source]).wait()
        first = (a * ROW_TILES + b // 2) * COL_TILES + b % 2 * COLS
        key_block = kv_in[source, 0].astype(jnp.float32).reshape(TILE_H, COLS, TILE_W, HD)
        value_block = kv_in[source, 1].astype(jnp.float32).reshape(TILE_H, COLS, TILE_W, HD)
        for c in range(COLS):
            k_tiles[first + c, f] = key_block[:, c].reshape(64, HD).astype(jnp.bfloat16)
            v_tiles[first + c, f, :, :HD] = (
                value_block[:, c].reshape(64, HD).astype(jnp.bfloat16)
            )

    factor = HD ** (-0.5) * math.log2(math.e)

    @pl.loop(0, layers * BY)
    def _(n):
        a, b = group_step(n)
        a, b = (layer + layers - a) % layers, (lane + BY - b) % BY
        group = a * BY + b
        pltpu.make_async_copy(q_in.at[group], q_in.at[group], q_sems.at[group]).wait()
        q_wide[...] = q_in[group].astype(jnp.float32).reshape(FT, TILE_H, COLS, TILE_W, HD)

        @pl.loop(0, COLS)
        def _(c):
            row, col = b // 2, b % 2 * COLS + c
            own = (a * ROW_TILES + row) * COL_TILES + col
            query = q_wide[:, :, c].reshape(TOKENS, HD).astype(jnp.bfloat16)
            scores, picks = [], []
            for w in range(windows):
                ka, kr, kc = a + off_ref[0, w], row + off_ref[1, w], col + off_ref[2, w]
                live = (ka >= 0) & (ka < layers) & (kr >= 0) & (kr < ROW_TILES)
                live = live & (kc >= 0) & (kc < COL_TILES)
                tile = (ka * ROW_TILES + kr) * COL_TILES + kc
                picks.append(jnp.where(live, tile, tiles))
                keys = k_tiles[jnp.where(live, tile, own)].reshape(TOKENS, HD)
                scores.append(
                    lax.dot_general(
                        query, keys, (((1,), (1,)), ((), ())),
                        preferred_element_type=jnp.float32,
                    )
                )
            top = functools.reduce(jnp.maximum, scores)
            top = jnp.max(top, axis=-1, keepdims=True)
            total = jnp.zeros((TOKENS, 2 * HD), jnp.float32)
            for score, pick in zip(scores, picks):
                raised = jnp.exp2((score - top) * factor).astype(jnp.bfloat16)
                values = v_tiles[pick].reshape(TOKENS, 2 * HD)
                total += jnp.dot(raised, values, preferred_element_type=jnp.float32)
            mixed = total[:, :HD] / total[:, HD:]
            o_wide[:, :, c] = mixed.reshape(FT, TILE_H, TILE_W, HD)

        o_buf[group] = o_wide[...].reshape(FT, 192, HD).astype(jnp.bfloat16)

        @pl.loop(0, FT)
        def _(f):
            to = device_of(a, f, b)

            @pl.when(to == me)
            def _():
                pltpu.make_async_copy(
                    o_buf.at[group, f], out_ref.at[:, columns(me)], out_sem
                ).start()

            @pl.when(to != me)
            def _():
                pltpu.make_async_remote_copy(
                    src_ref=o_buf.at[group, f],
                    dst_ref=out_ref.at[:, columns(me)],
                    send_sem=o_sent,
                    recv_sem=out_sem,
                    device_id=mesh_id(to),
                    device_id_type=pl.DeviceIdType.MESH,
                ).start()

    others = pl.ds(0, devices - 1)
    pltpu.make_async_copy(kv_in.at[others], kv_in.at[others], kv_sent).wait()
    sent = kv_in.at[others, 0]
    pltpu.make_async_copy(sent, sent, q_sent).wait()
    pltpu.make_async_copy(sent, sent, o_sent).wait()
    pltpu.make_async_copy(out_ref, out_ref, out_sem).wait()


def by_head(query_rows, key_rows, value_rows, window_offsets):
    shape = query_rows.shape
    devices = lax.axis_size("slab") * lax.axis_size("strip")
    layers = devices // (FT * BY)
    tiles = layers * ROW_TILES * COL_TILES
    windows = window_offsets.shape[0]
    tokens, width = shape[0] * shape[1], shape[2]
    flat = [x.reshape(tokens, width) for x in (query_rows, key_rows, value_rows)]
    pairs = tiles * windows * TOKENS * TOKENS
    out = pl.pallas_call(
        functools.partial(head_kernel, layers, windows),
        out_shape=pltpu.VMEM((tokens, width), jnp.bfloat16),
        in_specs=[pl.BlockSpec(memory_space=pltpu.SMEM)]
        + [pl.BlockSpec(memory_space=pl.ANY)] * 3,
        out_specs=pl.BlockSpec(memory_space=pl.ANY),
        scratch_shapes=[
            pltpu.VMEM((devices, 2, tokens, HD), jnp.bfloat16),
            pltpu.VMEM((layers * BY, FT, tokens, HD), jnp.bfloat16),
            pltpu.VMEM((layers * BY, FT, tokens, HD), jnp.bfloat16),
            pltpu.VMEM((tiles, FT, 64, HD), jnp.bfloat16),
            pltpu.VMEM((tiles + 1, FT, 64, 2 * HD), jnp.bfloat16),
            pltpu.VMEM((FT, TILE_H, COLS, TILE_W, HD), jnp.float32),
            pltpu.VMEM((FT, TILE_H, COLS, TILE_W, HD), jnp.float32),
            pltpu.SemaphoreType.DMA((devices,)),
            pltpu.SemaphoreType.DMA((layers * BY,)),
            pltpu.SemaphoreType.DMA,
            pltpu.SemaphoreType.DMA,
            pltpu.SemaphoreType.DMA,
            pltpu.SemaphoreType.DMA,
        ],
        compiler_params=pltpu.CompilerParams(
            collective_id=0, has_side_effects=True, vmem_limit_bytes=60 * 2**20
        ),
        cost_estimate=pl.CostEstimate(
            flops=6 * pairs * HD, bytes_accessed=8 * tokens * width, transcendentals=pairs
        ),
    )(window_offsets.T, *flat)
    return out.reshape(shape)


def solution(mesh):
    specs = P("slab", "strip", None)

    def attention(query_rows, key_rows, value_rows, window_offsets):
        slabs, strips = mesh.shape["slab"], mesh.shape["strip"]
        lines, width, features = query_rows.shape
        fits = slabs * strips * HD == features and lines == slabs * TILE_H
        fits = fits and strips == 2 and width == strips * COLS * TILE_W and slabs % 8 == 0
        return jax.shard_map(
            by_head if fits else per_device,
            mesh=mesh,
            in_specs=(specs, specs, specs, P()),
            out_specs=specs,
            check_vma=False,
        )(query_rows, key_rows, value_rows, window_offsets)

    return attention
```
